32 devices in a mesh: slide: 2 (over y), row: 4 (over z), col: 4 (over x, core).
Axes of the slice: x: 2, y: 2, z: 4, core: 2. Of those that a mesh axis runs over, the one named last changes fastest.
Arguments:
- tokens: bfloat16 [256, 256, 512], P(('slide', 'row'), 'col'), parts along dimension 0, may hold values from -6 to 6
- tissue_list: int32 [8, 4, 24], P('slide'), parts along dimension 0, may hold values from -1 to 31, as said below
- ln_gain: float32 [512], replicated, may hold values from 0.1 to 1.9
- w_qkv: bfloat16 [512, 1536], replicated, may hold values from -16 to 16
- w_out: bfloat16 [512, 512], replicated, may hold values from -2 to 2
- conv_weight: float32 [7, 7, 512], replicated, may hold values from -0.875 to 0.875
- conv_bias: float32 [512], replicated, may hold values from -4 to 4
- conv_gain: float32 [512], replicated, may hold values from 0.1 to 1.9
Outputs:
- encoded: bfloat16 [256, 256, 512], P(('slide', 'row'), 'col'), parts along dimension 0
The draws below stay inside these ranges and needn't reach their ends.
There are 2 independent parts, one for each index of `slide`. The reference program is written for one: setup_inputs(seed, part) draws one part's arguments, and reference() takes and returns one part's arrays. A program takes and returns all parts, laid end to end along the dimension named above; an argument that names none is the same for every part. Nothing has to cross between parts.
Inputs may be any that keep to these rules, and one draw needn't show every extreme that they name: `tissue_list`: each tile's list holds distinct local block numbers (block row * 8 + block column) first, then -1 entries; it names at least one block, and some tile names 24 blocks.
All inputs are finite; a program needn't handle non-finite values.
Results may differ from the reference program's by a relative error of at most 0.0063.
Values may be sent and summed in bfloat16 or wider, within the bound.
A program may use at most 128 MiB of HBM per device.

```python
import jax
import jax.numpy as jnp
from jax import lax

D = 512
HEADS = 8
BLK = 8
BR = 4
BC = 8
TCAP = 24
TILES_R = 4
TILES_C = 4
H_TOK = 128
W_TOK = 256


def draw_tissue_list(key, part):
    base = jax.random.fold_in(key, 7)
    key_count, key_full, key_perm = jax.random.split(base, 3)
    tiles = TILES_R * TILES_C
    counts = jax.random.randint(key_count, (tiles,), 1, TCAP + 1)
    fullest = jax.random.randint(key_full, (), 0, tiles)
    counts = jnp.where(jnp.arange(tiles) == fullest, TCAP, counts)
    perm_keys = jax.random.split(key_perm, tiles)
    orders = jax.vmap(lambda k: jax.random.permutation(k, BR * BC))(perm_keys)[:, :TCAP]
    listed = jnp.where(jnp.arange(TCAP)[None, :] < counts[:, None], orders, -1)
    return listed.reshape(TILES_R, TILES_C, TCAP).astype(jnp.int32)


def draw_w_qkv(key, part):
    base = jax.random.fold_in(key, 11)
    key_q, key_n, key_v = jax.random.split(base, 3)
    spread = D ** (-0.5)
    values = jax.random.normal(key_v, (D, D), jnp.float32) * spread
    query = jax.random.normal(key_q, (D, D), jnp.float32) * spread
    keys = jax.random.normal(key_n, (D, D), jnp.float32) * spread
    whole = jnp.concatenate([query, keys, values], axis=1)
    return jnp.clip(whole, -16.0, 16.0).astype(jnp.bfloat16)


def steps_of(stream_key, dims, shards, smallest, largest):
    def one(dim, blocks):
        steps = jax.random.uniform(jax.random.fold_in(jax.random.fold_in(stream_key, 6), dim), (blocks,), jnp.float32, smallest / len(shards), largest / len(shards))
        return jnp.repeat(jnp.exp(steps), dims[dim] // blocks).reshape((-1,) + (1,) * (len(dims) - dim - 1))

    level = one(*shards[0])
    for cut in shards[1:]:
        level = level * one(*cut)
    return level


def normal_values(stream_key, dims, scale, most, cuts=(), kind=jnp.bfloat16):
    values = jax.random.normal(stream_key, dims, jnp.float32) * scale
    if len(cuts) > 0:
        values = steps_of(stream_key, dims, cuts, -0.22, 0.18) * values
    return jnp.clip(values, min=-most, max=most).astype(kind)


def setup_inputs(seed: int = 0, part: int = 0) -> dict:
    seeds = jax.random.split(jax.random.key(seed), 9)
    own_keys = jax.random.split(jax.random.fold_in(seeds[8], part), 9)
    return {
        "tokens": normal_values(own_keys[0], (H_TOK, W_TOK, D), 1.0, 6.0, ((0, 4), (1, 4))),
        "tissue_list": draw_tissue_list(jax.random.fold_in(jax.random.fold_in(seeds[8], part), 71), part),
        "ln_gain": jnp.clip(1.0 + 0.18 * jax.random.normal(seeds[2], (D,), jnp.float32), 0.1, 1.9),
        "w_qkv": draw_w_qkv(jax.random.fold_in(seeds[8], 71), part),
        "w_out": normal_values(seeds[4], (D, D), (D // 64) ** -0.5, 2.0),
        "conv_weight": normal_values(seeds[5], (7, 7, D), 49 ** -0.5, 0.875, (), jnp.float32),
        "conv_bias": normal_values(seeds[6], (D,), 1.0, 4.0, (), jnp.float32),
        "conv_gain": jnp.clip(1.0 + 0.18 * jax.random.normal(seeds[7], (D,), jnp.float32), 0.1, 1.9),
    }


def layer_norm(values, gain):
    mean = lax.optimization_barrier(jnp.mean(values, axis=-1, keepdims=True))
    centred = values - mean
    variance = lax.optimization_barrier(jnp.mean(centred * centred, axis=-1, keepdims=True))
    return centred * lax.rsqrt(variance + 1e-06) * gain

def block_table(tissue_list):
    tiles_r, tiles_c, slots = tissue_list.shape
    hits = jnp.any(tissue_list[..., None] == jnp.arange(BR * BC, dtype=jnp.int32), axis=2)
    hits = hits.reshape(tiles_r, tiles_c, BR, BC).transpose(0, 2, 1, 3)
    return hits.reshape(tiles_r * BR, tiles_c * BC)

def attend(query, keys, values, key_ok):
    rows = query.shape[0]
    span = keys.shape[0]
    head_dim = query.shape[1] // HEADS
    qh = query.reshape(rows, HEADS, head_dim).astype(jnp.float32)
    kh = keys.reshape(span, HEADS, head_dim).astype(jnp.float32)
    vh = values.reshape(span, HEADS, head_dim).astype(jnp.float32)
    scores = jnp.einsum('rhd,shd->hrs', qh, kh) * head_dim ** (-0.5)
    scores = jnp.where(key_ok[None, None, :], scores, -1e+30)
    top = lax.optimization_barrier(jnp.max(scores, axis=-1, keepdims=True))
    weights = jnp.exp(scores - top)
    probs = (weights / lax.optimization_barrier(jnp.sum(weights, axis=-1, keepdims=True))).astype(jnp.bfloat16)
    out = jnp.einsum('hrs,shd->rhd', probs.astype(jnp.float32), vh)
    return out.reshape(rows, HEADS * head_dim).astype(jnp.bfloat16)

def reference(tokens, tissue_list, ln_gain, w_qkv, w_out, conv_weight, conv_bias, conv_gain):
    height, breadth, width = tokens.shape
    block_rows = height // BLK
    block_cols = breadth // BLK
    anchor = jnp.zeros((), jnp.int32)
    row_groups = tokens.reshape(block_rows, BLK, breadth, width)

    def project(group):
        normed = layer_norm(group.astype(jnp.float32), ln_gain).astype(jnp.bfloat16)
        flat = jnp.dot(normed.reshape(-1, width), w_qkv, preferred_element_type=jnp.float32)
        return flat.astype(jnp.bfloat16).reshape(BLK, breadth, 3 * width)
    projected = lax.map(project, row_groups).reshape(height, breadth, 3 * width)
    query = projected[..., :width]
    pairs = jnp.pad(projected[..., width:], ((BLK, BLK), (BLK, BLK), (0, 0)))
    table = block_table(tissue_list)
    near_table = jnp.pad(table, 1)

    def one_block(bi, bj):
        top_row = (bi * BLK).astype(jnp.int32)
        left_col = (bj * BLK).astype(jnp.int32)
        query_block = lax.dynamic_slice(query, (top_row, left_col, anchor), (BLK, BLK, width)).reshape(BLK * BLK, width)
        window = lax.dynamic_slice(pairs, (top_row, left_col, anchor), (3 * BLK, 3 * BLK, 2 * width))
        window = window.reshape(9 * BLK * BLK, 2 * width)
        beside_all = lax.dynamic_slice(near_table, (bi.astype(jnp.int32), bj.astype(jnp.int32)), (3, 3))
        key_ok = jnp.repeat(jnp.repeat(beside_all, BLK, 0), BLK, 1).reshape(-1)
        out = attend(query_block, window[:, :width], window[:, width:], key_ok)
        return jnp.dot(out, w_out, preferred_element_type=jnp.float32)

    def block_row(bi):
        deltas = jax.vmap(lambda bj: one_block(bi, bj))(jnp.arange(block_cols, dtype=jnp.int32))
        gate = lax.dynamic_slice(table, (bi.astype(jnp.int32), anchor), (1, block_cols))[0]
        deltas = jnp.where(gate[:, None, None], deltas, 0.0)
        deltas = deltas.reshape(block_cols, BLK, BLK, width).transpose(1, 0, 2, 3).reshape(BLK, breadth, width)
        rows_in = lax.dynamic_slice(tokens, ((bi * BLK).astype(jnp.int32), anchor, anchor), (BLK, breadth, width))
        return (rows_in.astype(jnp.float32) + deltas).astype(jnp.bfloat16)
    mixed = lax.map(block_row, jnp.arange(block_rows, dtype=jnp.int32)).reshape(height, breadth, width)
    framed = jnp.pad(mixed, ((3, 3), (3, 3), (0, 0)))
    filtered = jnp.zeros((height, breadth, width), jnp.float32)
    for dy in range(7):
        for dx in range(7):
            filtered = filtered + framed[dy:dy + height, dx:dx + breadth].astype(jnp.float32) * conv_weight[dy, dx]
    filtered = filtered + conv_bias
    branch = layer_norm(filtered, conv_gain)
    return (mixed.astype(jnp.float32) + branch).astype(jnp.bfloat16)
```

```python
import functools

import jax
import jax.numpy as jnp
from jax import lax
from jax.experimental import pallas as pl
from jax.experimental.pallas import tpu as pltpu
from jax.sharding import PartitionSpec as P

HEADS = 8
BLK = 8
BR = 4
BC = 8
GROUP = 4
SIDES = ((-1, 0), (1, 0), (0, -1), (0, 1), (-1, -1), (-1, 1), (1, -1), (1, 1))
VM = pl.BlockSpec(memory_space=pltpu.VMEM)
SM = pl.BlockSpec(memory_space=pltpu.SMEM)
ANY = pl.BlockSpec(memory_space=pl.ANY)
MIB = 1024 * 1024


def block_table(tissue_list):
    tiles_r, tiles_c, slots = tissue_list.shape
    hits = jnp.any(tissue_list[..., None] == jnp.arange(BR * BC, dtype=jnp.int32), axis=2)
    hits = hits.reshape(tiles_r, tiles_c, BR, BC).transpose(0, 2, 1, 3)
    return hits.reshape(tiles_r * BR, tiles_c * BC)


def exchange(sizes, views, send_sems, recv_sems):
    n_r, n_c = sizes
    r, c = lax.axis_index("row"), lax.axis_index("col")
    barrier = pltpu.get_barrier_semaphore()

    def there(dr, dc):
        ok = None
        for at, step, n in ((r, dr, n_r), (c, dc, n_c)):
            if step == -1:
                one = at > 0
            elif step == 1:
                one = at < n - 1
            else:
                continue
            ok = one if ok is None else jnp.logical_and(ok, one)
        return ok

    def target(dr, dc):
        return {"row": r + dr, "col": c + dc}

    for dr, dc in SIDES:
        @pl.when(there(dr, dc))
        def _():
            pl.semaphore_signal(
                barrier, inc=1, device_id=target(dr, dc), device_id_type=pl.DeviceIdType.MESH
            )

    peers = sum(there(dr, dc).astype(jnp.int32) for dr, dc in SIDES)
    pl.semaphore_wait(barrier, peers)

    def copy(k):
        dr, dc = SIDES[k]
        src, dst = views(dr, dc)
        return pltpu.make_async_remote_copy(
            src_ref=src,
            dst_ref=dst,
            send_sem=send_sems.at[k],
            recv_sem=recv_sems.at[k],
            device_id=target(dr, dc),
            device_id_type=pl.DeviceIdType.MESH,
        )

    for k, (dr, dc) in enumerate(SIDES):
        @pl.when(there(dr, dc))
        def _():
            copy(k).start()

    def finish():
        for k, (dr, dc) in enumerate(SIDES):
            @pl.when(there(dr, dc))
            def _():
                copy(k).wait_send()

            @pl.when(there(-dr, -dc))
            def _():
                copy(k).wait_recv()

    return finish


def token_halo_kernel(sizes, blocks, frame, send_sems, recv_sems, own_sem):
    def span(step, n):
        if step == -1:
            return pl.ds(0, 1), pl.ds(n + 1, 1)
        if step == 1:
            return pl.ds(n - 1, 1), pl.ds(0, 1)
        return pl.ds(0, n), pl.ds(1, n)

    def views(dr, dc):
        (sr, tr), (sc, tc) = span(dr, BR), span(dc, BC)
        return blocks.at[sr, sc], frame.at[tr, tc]

    own = pltpu.make_async_copy(blocks, frame.at[pl.ds(1, BR), pl.ds(1, BC)], own_sem)
    own.start()
    finish = exchange(sizes, views, send_sems, recv_sems)
    own.wait()
    finish()


def mixed_halo_kernel(
    sizes, mixed, edges, top, bottom, sides, corners, send_sems, recv_sems
):
    height = mixed.shape[0]
    tall = edges.shape[1]

    def views(dr, dc):
        if dc == 0:
            if dr == -1:
                return mixed.at[pl.ds(0, 3)], bottom
            return mixed.at[pl.ds(height - 3, 3)], top
        mine = 0 if dc == -1 else 1
        if dr == 0:
            return edges.at[mine], sides.at[1 - mine]
        rows = pl.ds(0, 32) if dr == -1 else pl.ds(tall - 32, 32)
        place = (2 if dr == -1 else 0) + 1 - mine
        return edges.at[mine, rows], corners.at[place]

    exchange(sizes, views, send_sems, recv_sems)()


def attention_kernel(
    ok_ref, frame, gain, w_qkv, w_out, bias, mixed, edges, qkv, normed, att, mix
):
    width = frame.shape[-1]
    tok = BLK * BLK
    half = width // 2
    head = width // HEADS

    def project(i, carry):
        for j in range(BC + 2):
            x = frame[i, j].astype(jnp.float32)
            x = jnp.where(ok_ref[i, j] != 0, x, 0.0)
            cent = x - jnp.mean(x, axis=-1, keepdims=True)
            var = jnp.mean(cent * cent, axis=-1, keepdims=True)
            y = cent * lax.rsqrt(var + 1e-06) * gain[...]
            normed[pl.ds(j * tok, tok), :] = y.astype(jnp.bfloat16)
        for n in range(3):
            cols = pl.ds(n * width, width)
            p = jnp.dot(normed[...], w_qkv[:, cols], preferred_element_type=jnp.float32)
            qkv[i, :, :, cols] = p.astype(jnp.bfloat16).reshape(BC + 2, tok, width)
        return carry

    lax.fori_loop(0, BR + 2, project, 0)

    shape = (GROUP * tok, half)
    same = (
        lax.broadcasted_iota(jnp.int32, shape, 0) // tok
        == lax.broadcasted_iota(jnp.int32, shape, 1) // head
    )

    def attend(b, carry):
        bi = b // BC
        bj = b % BC
        ok = ok_ref[bi + 1, bj + 1] != 0

        @pl.when(ok)
        def _():
            for g in range(2):
                q = qkv[bi + 1, bj + 1, :, pl.ds(g * half, half)].astype(jnp.float32)
                q = q * head ** (-0.5)
                q = jnp.where(same, jnp.concatenate([q] * GROUP, axis=0), 0.0)
                q = q.astype(jnp.bfloat16)

                def window(start):
                    return jnp.concatenate(
                        [
                            qkv[bi + a, pl.ds(bj, 3), :, pl.ds(start, half)].reshape(
                                3 * tok, half
                            )
                            for a in range(3)
                        ],
                        axis=0,
                    )

                s = lax.dot_general(
                    q,
                    window(width + g * half),
                    (((1,), (1,)), ((), ())),
                    preferred_element_type=jnp.float32,
                )
                s = s + bias[b]
                e = jnp.exp(s - jnp.max(s, axis=-1, keepdims=True))
                total = jnp.sum(e, axis=-1, keepdims=True)
                o = jnp.dot(
                    e.astype(jnp.bfloat16),
                    window(2 * width + g * half),
                    preferred_element_type=jnp.float32,
                )
                o = jnp.where(same, o * (1.0 / total), 0.0)
                o = o[:tok] + o[tok : 2 * tok] + o[2 * tok : 3 * tok] + o[3 * tok :]
                att[b, :, pl.ds(g * half, half)] = o.astype(jnp.bfloat16)

        @pl.when(jnp.logical_not(ok))
        def _():
            att[b] = jnp.zeros((tok, width), jnp.bfloat16)

        return carry

    lax.fori_loop(0, BR * BC, attend, 0)

    def out(bi, carry):
        a = att[pl.ds(bi * BC, BC)].reshape(BC * tok, width)
        d = jnp.dot(a, w_out[...], preferred_element_type=jnp.float32)
        rows = pl.ds(bi * BLK, BLK)
        for bj in range(BC):
            m = frame[bi + 1, bj + 1].astype(jnp.float32) + d[bj * tok : (bj + 1) * tok]
            mix[rows, pl.ds(bj * BLK, BLK), :] = m.reshape(BLK, BLK, width)
        mixed[rows] = mix[rows].astype(jnp.bfloat16)
        for side, start in ((0, 0), (1, (BC - 1) * BLK)):
            m = mix[rows, pl.ds(start, BLK), :].reshape(tok, width)
            edges[side, pl.ds(bi * tok, tok), :] = m.astype(jnp.bfloat16)
        return carry

    lax.fori_loop(0, BR, out, 0)


def conv_kernel(
    flags, mixed, top, bottom, sides, corners, weight, bias, gain, out, framed, filt
):
    height, breadth, width = mixed.shape
    up, down, left, right = [flags[k] != 0 for k in range(4)]
    f32 = jnp.float32

    def fill(i, carry):
        rows = pl.ds(i * BLK, BLK)
        framed[pl.ds(i * BLK + 3, BLK), pl.ds(8, breadth), :] = mixed[rows].astype(f32)
        for k, ok, start in ((0, left, 0), (1, right, breadth + 8)):
            v = sides[k, pl.ds(i * BLK * 8, BLK * 8), :].astype(f32)
            framed[pl.ds(i * BLK + 3, BLK), pl.ds(start, 8), :] = jnp.where(ok, v, 0.0).reshape(
                BLK, 8, width
            )
        return carry

    lax.fori_loop(0, height // BLK, fill, 0)
    for k, ok, ref, start in ((0, up, top, 0), (2, down, bottom, height + 3)):
        rows = pl.ds(start, 3)
        framed[rows, pl.ds(8, breadth), :] = jnp.where(ok, ref[...].astype(f32), 0.0)
        for h, side_ok, col in ((0, left, 0), (1, right, breadth + 8)):
            v = corners[k + h].astype(f32).reshape(4, 8, width)
            v = v[1:] if k == 0 else v[:3]
            both = jnp.logical_and(ok, side_ok)
            framed[rows, pl.ds(col, 8), :] = jnp.where(both, v, 0.0)

    def row_block(i, carry):
        r0 = i * BLK

        def lanes(l, inner):
            lane = pl.ds(pl.multiple_of(l * 128, 128), 128)
            for c0 in range(0, breadth, 8):
                acc = jnp.zeros((BLK, 8, 128), f32) + bias[:, lane]
                for dx in range(7):
                    v = framed[pl.ds(r0, BLK + 6), pl.ds(c0 + dx + 5, 8), lane]
                    for dy in range(7):
                        acc = acc + v[dy : dy + BLK] * weight[dy * 7 + dx, :, lane]
                filt[:, pl.ds(c0, 8), lane] = acc
            return inner

        lax.fori_loop(0, width // 128, lanes, 0)

        def norm(y, inner):
            f = filt[y]
            cent = f - jnp.mean(f, axis=-1, keepdims=True)
            var = jnp.mean(cent * cent, axis=-1, keepdims=True)
            branch = cent * lax.rsqrt(var + 1e-06) * gain[...]
            out[r0 + y] = (mixed[r0 + y].astype(f32) + branch).astype(jnp.bfloat16)
            return inner

        lax.fori_loop(0, BLK, norm, 0)
        return carry

    lax.fori_loop(0, height // BLK, row_block, 0)


def per_device(tokens, tissue_list, ln_gain, w_qkv, w_out, conv_weight, conv_bias, conv_gain):
    height, breadth, width = tokens.shape
    tok = BLK * BLK
    bf16, f32 = jnp.bfloat16, jnp.float32
    sizes = (lax.axis_size("row"), lax.axis_size("col"))
    row, col = lax.axis_index("row"), lax.axis_index("col")
    dma = pltpu.SemaphoreType.DMA

    blocks = tokens.reshape(BR, BLK, BC, BLK, width).transpose(0, 2, 1, 3, 4)
    blocks = blocks.reshape(BR, BC, tok, width)
    frame = pl.pallas_call(
        functools.partial(token_halo_kernel, sizes),
        out_shape=jax.ShapeDtypeStruct((BR + 2, BC + 2, tok, width), bf16),
        in_specs=[ANY],
        out_specs=ANY,
        scratch_shapes=[dma((8,)), dma((8,)), dma],
        compiler_params=pltpu.CompilerParams(collective_id=0, has_side_effects=True),
    )(blocks)

    table = jnp.pad(block_table(tissue_list), 1)
    near = lax.dynamic_slice(table, (row * BR, col * BC), (BR + 2, BC + 2))
    okay = jnp.stack(
        [near[a : a + BR, b : b + BC] for a in range(3) for b in range(3)], axis=-1
    ).reshape(BR * BC, 1, 9)
    bias = jnp.repeat(jnp.where(okay, 0.0, -1e30).astype(f32), tok, axis=-1)

    mixed, edges = pl.pallas_call(
        attention_kernel,
        out_shape=(
            jax.ShapeDtypeStruct((height, breadth, width), bf16),
            jax.ShapeDtypeStruct((2, height * 8, width), bf16),
        ),
        in_specs=[SM, VM, VM, VM, VM, VM],
        out_specs=(VM, VM),
        scratch_shapes=[
            pltpu.VMEM((BR + 2, BC + 2, tok, 3 * width), bf16),
            pltpu.VMEM(((BC + 2) * tok, width), bf16),
            pltpu.VMEM((BR * BC, tok, width), bf16),
            pltpu.VMEM((height, breadth, width), f32),
        ],
        compiler_params=pltpu.CompilerParams(vmem_limit_bytes=50 * MIB),
    )(near.astype(jnp.int32), frame, ln_gain.reshape(1, width), w_qkv, w_out, bias)

    top, bottom, sides, corners = pl.pallas_call(
        functools.partial(mixed_halo_kernel, sizes),
        out_shape=(
            jax.ShapeDtypeStruct((3, breadth, width), bf16),
            jax.ShapeDtypeStruct((3, breadth, width), bf16),
            jax.ShapeDtypeStruct((2, height * 8, width), bf16),
            jax.ShapeDtypeStruct((4, 32, width), bf16),
        ),
        in_specs=[ANY, ANY],
        out_specs=(ANY,) * 4,
        scratch_shapes=[dma((8,)), dma((8,))],
        compiler_params=pltpu.CompilerParams(collective_id=1, has_side_effects=True),
    )(mixed, edges)

    flags = jnp.stack([row > 0, row < sizes[0] - 1, col > 0, col < sizes[1] - 1])
    weight = jnp.broadcast_to(conv_weight.reshape(49, 1, width), (49, 8, width))
    return pl.pallas_call(
        conv_kernel,
        out_shape=jax.ShapeDtypeStruct((height, breadth, width), bf16),
        in_specs=[SM] + [VM] * 8,
        out_specs=VM,
        scratch_shapes=[
            pltpu.VMEM((height + 6, breadth + 16, width), f32),
            pltpu.VMEM((BLK, breadth, width), f32),
        ],
        compiler_params=pltpu.CompilerParams(vmem_limit_bytes=40 * MIB),
    )(
        flags.astype(jnp.int32),
        mixed,
        top,
        bottom,
        sides,
        corners,
        weight,
        conv_bias.reshape(1, width),
        conv_gain.reshape(1, width),
    )


def solution(mesh):
    tile = P(("slide", "row"), "col", None)
    in_specs = (tile, P("slide", None, None), P(), P(), P(), P(), P(), P())
    return jax.shard_map(
        per_device, mesh=mesh, in_specs=in_specs, out_specs=tile, check_vma=False
    )
```

```python
import functools

import jax
import jax.numpy as jnp
from jax import lax
from jax.experimental import pallas as pl
from jax.experimental.pallas import tpu as pltpu
from jax.sharding import PartitionSpec as P

HEADS = 8
BLK = 8
BR = 4
BC = 8
GROUP = 4
SIDES = ((-1, 0), (1, 0), (0, -1), (0, 1), (-1, -1), (-1, 1), (1, -1), (1, 1))
VM = pl.BlockSpec(memory_space=pltpu.VMEM)
SM = pl.BlockSpec(memory_space=pltpu.SMEM)
ANY = pl.BlockSpec(memory_space=pl.ANY)
MIB = 1024 * 1024


def block_table(tissue_list):
    tiles_r, tiles_c, slots = tissue_list.shape
    hits = jnp.any(tissue_list[..., None] == jnp.arange(BR * BC, dtype=jnp.int32), axis=2)
    hits = hits.reshape(tiles_r, tiles_c, BR, BC).transpose(0, 2, 1, 3)
    return hits.reshape(tiles_r * BR, tiles_c * BC)


def exchange(sizes, views, send_sems, recv_sems):
    n_r, n_c = sizes
    r, c = lax.axis_index("row"), lax.axis_index("col")
    barrier = pltpu.get_barrier_semaphore()

    def there(dr, dc):
        ok = None
        for at, step, n in ((r, dr, n_r), (c, dc, n_c)):
            if step == -1:
                one = at > 0
            elif step == 1:
                one = at < n - 1
            else:
                continue
            ok = one if ok is None else jnp.logical_and(ok, one)
        return ok

    def target(dr, dc):
        return {"row": r + dr, "col": c + dc}

    for dr, dc in SIDES:
        @pl.when(there(dr, dc))
        def _():
            pl.semaphore_signal(
                barrier, inc=1, device_id=target(dr, dc), device_id_type=pl.DeviceIdType.MESH
            )

    peers = sum(there(dr, dc).astype(jnp.int32) for dr, dc in SIDES)
    pl.semaphore_wait(barrier, peers)

    def copy(k):
        dr, dc = SIDES[k]
        src, dst = views(dr, dc)
        return pltpu.make_async_remote_copy(
            src_ref=src,
            dst_ref=dst,
            send_sem=send_sems.at[k],
            recv_sem=recv_sems.at[k],
            device_id=target(dr, dc),
            device_id_type=pl.DeviceIdType.MESH,
        )

    for k, (dr, dc) in enumerate(SIDES):
        @pl.when(there(dr, dc))
        def _():
            copy(k).start()

    def finish():
        for k, (dr, dc) in enumerate(SIDES):
            @pl.when(there(dr, dc))
            def _():
                copy(k).wait_send()

            @pl.when(there(-dr, -dc))
            def _():
                copy(k).wait_recv()

    return finish


def token_halo_kernel(sizes, blocks, frame, send_sems, recv_sems):
    def span(step, n):
        if step == -1:
            return pl.ds(0, 1), pl.ds(n + 1, 1)
        if step == 1:
            return pl.ds(n - 1, 1), pl.ds(0, 1)
        return pl.ds(0, n), pl.ds(1, n)

    def views(dr, dc):
        (sr, tr), (sc, tc) = span(dr, BR), span(dc, BC)
        return blocks.at[sr, sc], frame.at[tr, tc]

    exchange(sizes, views, send_sems, recv_sems)()


def mixed_halo_kernel(
    sizes, mixed, edges, top, bottom, sides, corners, send_sems, recv_sems
):
    height = mixed.shape[0]
    tall = edges.shape[1]

    def views(dr, dc):
        if dc == 0:
            if dr == -1:
                return mixed.at[pl.ds(0, 3)], bottom
            return mixed.at[pl.ds(height - 3, 3)], top
        mine = 0 if dc == -1 else 1
        if dr == 0:
            return edges.at[mine], sides.at[1 - mine]
        rows = pl.ds(0, 32) if dr == -1 else pl.ds(tall - 32, 32)
        place = (2 if dr == -1 else 0) + 1 - mine
        return edges.at[mine, rows], corners.at[place]

    exchange(sizes, views, send_sems, recv_sems)()


def attention_kernel(
    ok_ref, blocks, frame, gain, w_qkv, w_out, bias, mixed, edges, qkv, normed, att, mix
):
    width = frame.shape[-1]
    tok = BLK * BLK
    half = width // 2
    head = width // HEADS

    def norm(x, at):
        cent = x - jnp.mean(x, axis=-1, keepdims=True)
        var = jnp.mean(cent * cent, axis=-1, keepdims=True)
        y = cent * lax.rsqrt(var + 1e-06) * gain[...]
        normed[pl.ds(at * tok, tok), :] = y.astype(jnp.bfloat16)

    def halo(i, j):
        x = frame[i, j].astype(jnp.float32)
        return jnp.where(ok_ref[i, j] != 0, x, 0.0)

    def own_row(i, carry):
        for j in range(BC):
            norm(blocks[i, j].astype(jnp.float32), j + 1)
        norm(halo(i + 1, 0), 0)
        norm(halo(i + 1, BC + 1), BC + 1)
        for n in range(3):
            cols = pl.ds(n * width, width)
            p = jnp.dot(normed[...], w_qkv[:, cols], preferred_element_type=jnp.float32)
            qkv[i + 1, :, :, cols] = p.astype(jnp.bfloat16).reshape(BC + 2, tok, width)
        return carry

    lax.fori_loop(0, BR, own_row, 0)

    def halo_row(t, carry):
        i = t * (BR + 1)
        for j in range(BC + 2):
            norm(halo(i, j), j)
        for n in (1, 2):
            cols = pl.ds(n * width, width)
            p = jnp.dot(normed[...], w_qkv[:, cols], preferred_element_type=jnp.float32)
            qkv[i, :, :, cols] = p.astype(jnp.bfloat16).reshape(BC + 2, tok, width)
        return carry

    lax.fori_loop(0, 2, halo_row, 0)

    shape = (GROUP * tok, half)
    same = (
        lax.broadcasted_iota(jnp.int32, shape, 0) // tok
        == lax.broadcasted_iota(jnp.int32, shape, 1) // head
    )

    def attend(b, carry):
        bi = b // BC
        bj = b % BC
        ok = ok_ref[bi + 1, bj + 1] != 0

        @pl.when(ok)
        def _():
            for g in range(2):
                q = qkv[bi + 1, bj + 1, :, pl.ds(g * half, half)].astype(jnp.float32)
                q = q * head ** (-0.5)
                q = jnp.where(same, jnp.concatenate([q] * GROUP, axis=0), 0.0)
                q = q.astype(jnp.bfloat16)

                def window(start):
                    return jnp.concatenate(
                        [
                            qkv[bi + a, pl.ds(bj, 3), :, pl.ds(start, half)].reshape(
                                3 * tok, half
                            )
                            for a in range(3)
                        ],
                        axis=0,
                    )

                s = lax.dot_general(
                    q,
                    window(width + g * half),
                    (((1,), (1,)), ((), ())),
                    preferred_element_type=jnp.float32,
                )
                s = s + bias[b]
                e = jnp.exp(s - jnp.max(s, axis=-1, keepdims=True))
                total = jnp.sum(e, axis=-1, keepdims=True)
                o = jnp.dot(
                    e.astype(jnp.bfloat16),
                    window(2 * width + g * half),
                    preferred_element_type=jnp.float32,
                )
                o = jnp.where(same, o * (1.0 / total), 0.0)
                o = o[:tok] + o[tok : 2 * tok] + o[2 * tok : 3 * tok] + o[3 * tok :]
                att[b, :, pl.ds(g * half, half)] = o.astype(jnp.bfloat16)

        @pl.when(jnp.logical_not(ok))
        def _():
            att[b] = jnp.zeros((tok, width), jnp.bfloat16)

        return carry

    lax.fori_loop(0, BR * BC, attend, 0)

    def out(bi, carry):
        a = att[pl.ds(bi * BC, BC)].reshape(BC * tok, width)
        d = jnp.dot(a, w_out[...], preferred_element_type=jnp.float32)
        rows = pl.ds(bi * BLK, BLK)
        for bj in range(BC):
            m = blocks[bi, bj].astype(jnp.float32) + d[bj * tok : (bj + 1) * tok]
            mix[rows, pl.ds(bj * BLK, BLK), :] = m.reshape(BLK, BLK, width)
        mixed[rows] = mix[rows].astype(jnp.bfloat16)
        for side, start in ((0, 0), (1, (BC - 1) * BLK)):
            m = mix[rows, pl.ds(start, BLK), :].reshape(tok, width)
            edges[side, pl.ds(bi * tok, tok), :] = m.astype(jnp.bfloat16)
        return carry

    lax.fori_loop(0, BR, out, 0)


def conv_kernel(
    flags, mixed, top, bottom, sides, corners, weight, bias, gain, out, framed, filt
):
    height, breadth, width = mixed.shape
    up, down, left, right = [flags[k] != 0 for k in range(4)]
    f32 = jnp.float32
    chunks = width // 128

    def put(rows, cols, v):
        for l in range(chunks):
            framed[l, rows, cols, :] = v[..., l * 128 : (l + 1) * 128]

    def fill(i, carry):
        rows = pl.ds(i * BLK, BLK)
        into = pl.ds(i * BLK + 3, BLK)
        put(into, pl.ds(8, breadth), mixed[rows].astype(f32))
        for k, ok, start in ((0, left, 0), (1, right, breadth + 8)):
            v = sides[k, pl.ds(i * BLK * 8, BLK * 8), :].astype(f32)
            put(into, pl.ds(start, 8), jnp.where(ok, v, 0.0).reshape(BLK, 8, width))
        return carry

    lax.fori_loop(0, height // BLK, fill, 0)
    for k, ok, ref, start in ((0, up, top, 0), (2, down, bottom, height + 3)):
        rows = pl.ds(start, 3)
        put(rows, pl.ds(8, breadth), jnp.where(ok, ref[...].astype(f32), 0.0))
        for h, side_ok, col in ((0, left, 0), (1, right, breadth + 8)):
            v = corners[k + h].astype(f32).reshape(4, 8, width)
            v = v[1:] if k == 0 else v[:3]
            both = jnp.logical_and(ok, side_ok)
            put(rows, pl.ds(col, 8), jnp.where(both, v, 0.0))

    def row_block(i, carry):
        r0 = i * BLK

        def lanes(l, inner):
            for c0 in range(0, breadth, 8):
                acc = jnp.zeros((BLK, 8, 128), f32) + bias[l]
                for dx in range(7):
                    v = framed[l, pl.ds(r0, BLK + 6), pl.ds(c0 + dx + 5, 8), :]
                    for dy in range(7):
                        acc = acc + v[dy : dy + BLK] * weight[l, dy * 7 + dx]
                filt[l, :, pl.ds(c0, 8), :] = acc
            return inner

        lax.fori_loop(0, chunks, lanes, 0)

        def norm(y, inner):
            f = jnp.concatenate([filt[l, y] for l in range(chunks)], axis=-1)
            cent = f - jnp.mean(f, axis=-1, keepdims=True)
            var = jnp.mean(cent * cent, axis=-1, keepdims=True)
            branch = cent * lax.rsqrt(var + 1e-06) * gain[...]
            out[r0 + y] = (mixed[r0 + y].astype(f32) + branch).astype(jnp.bfloat16)
            return inner

        lax.fori_loop(0, BLK, norm, 0)
        return carry

    lax.fori_loop(0, height // BLK, row_block, 0)


def per_device(tokens, tissue_list, ln_gain, w_qkv, w_out, conv_weight, conv_bias, conv_gain):
    height, breadth, width = tokens.shape
    tok = BLK * BLK
    bf16, f32 = jnp.bfloat16, jnp.float32
    sizes = (lax.axis_size("row"), lax.axis_size("col"))
    row, col = lax.axis_index("row"), lax.axis_index("col")
    dma = pltpu.SemaphoreType.DMA

    blocks = tokens.reshape(BR, BLK, BC, BLK, width).transpose(0, 2, 1, 3, 4)
    blocks = blocks.reshape(BR, BC, tok, width)
    frame = pl.pallas_call(
        functools.partial(token_halo_kernel, sizes),
        out_shape=jax.ShapeDtypeStruct((BR + 2, BC + 2, tok, width), bf16),
        in_specs=[ANY],
        out_specs=ANY,
        scratch_shapes=[dma((8,)), dma((8,))],
        compiler_params=pltpu.CompilerParams(collective_id=0, has_side_effects=True),
    )(blocks)

    table = jnp.pad(block_table(tissue_list), 1)
    near = lax.dynamic_slice(table, (row * BR, col * BC), (BR + 2, BC + 2))
    okay = jnp.stack(
        [near[a : a + BR, b : b + BC] for a in range(3) for b in range(3)], axis=-1
    ).reshape(BR * BC, 1, 9)
    bias = jnp.repeat(jnp.where(okay, 0.0, -1e30).astype(f32), tok, axis=-1)

    mixed, edges = pl.pallas_call(
        attention_kernel,
        out_shape=(
            jax.ShapeDtypeStruct((height, breadth, width), bf16),
            jax.ShapeDtypeStruct((2, height * 8, width), bf16),
        ),
        in_specs=[SM] + [VM] * 6,
        out_specs=(VM, VM),
        scratch_shapes=[
            pltpu.VMEM((BR + 2, BC + 2, tok, 3 * width), bf16),
            pltpu.VMEM(((BC + 2) * tok, width), bf16),
            pltpu.VMEM((BR * BC, tok, width), bf16),
            pltpu.VMEM((height, breadth, width), f32),
        ],
        compiler_params=pltpu.CompilerParams(vmem_limit_bytes=50 * MIB),
    )(near.astype(jnp.int32), blocks, frame, ln_gain.reshape(1, width), w_qkv, w_out, bias)

    top, bottom, sides, corners = pl.pallas_call(
        functools.partial(mixed_halo_kernel, sizes),
        out_shape=(
            jax.ShapeDtypeStruct((3, breadth, width), bf16),
            jax.ShapeDtypeStruct((3, breadth, width), bf16),
            jax.ShapeDtypeStruct((2, height * 8, width), bf16),
            jax.ShapeDtypeStruct((4, 32, width), bf16),
        ),
        in_specs=[ANY, ANY],
        out_specs=(ANY,) * 4,
        scratch_shapes=[dma((8,)), dma((8,))],
        compiler_params=pltpu.CompilerParams(collective_id=1, has_side_effects=True),
    )(mixed, edges)

    flags = jnp.stack([row > 0, row < sizes[0] - 1, col > 0, col < sizes[1] - 1])
    chunks = width // 128
    weight = conv_weight.reshape(49, chunks, 1, 128).transpose(1, 0, 2, 3)
    weight = jnp.broadcast_to(weight, (chunks, 49, 8, 128))
    return pl.pallas_call(
        conv_kernel,
        out_shape=jax.ShapeDtypeStruct((height, breadth, width), bf16),
        in_specs=[SM] + [VM] * 8,
        out_specs=VM,
        scratch_shapes=[
            pltpu.VMEM((width // 128, height + 6, breadth + 16, 128), f32),
            pltpu.VMEM((width // 128, BLK, breadth, 128), f32),
        ],
        compiler_params=pltpu.CompilerParams(vmem_limit_bytes=40 * MIB),
    )(
        flags.astype(jnp.int32),
        mixed,
        top,
        bottom,
        sides,
        corners,
        weight,
        conv_bias.reshape(chunks, 1, 128),
        conv_gain.reshape(1, width),
    )


def solution(mesh):
    tile = P(("slide", "row"), "col", None)
    in_specs = (tile, P("slide", None, None), P(), P(), P(), P(), P(), P())
    return jax.shard_map(
        per_device, mesh=mesh, in_specs=in_specs, out_specs=tile, check_vma=False
    )
```

```python
import functools

import jax
import jax.numpy as jnp
from jax import lax
from jax.experimental import pallas as pl
from jax.experimental.pallas import tpu as pltpu
from jax.sharding import PartitionSpec as P

HEADS = 8
BLK = 8
BR = 4
BC = 8
GROUP = 4
SIDES = ((-1, 0), (1, 0), (0, -1), (0, 1), (-1, -1), (-1, 1), (1, -1), (1, 1))
VM = pl.BlockSpec(memory_space=pltpu.VMEM)
SM = pl.BlockSpec(memory_space=pltpu.SMEM)
ANY = pl.BlockSpec(memory_space=pl.ANY)
MIB = 1024 * 1024


def block_table(tissue_list):
    tiles_r, tiles_c, slots = tissue_list.shape
    hits = jnp.any(tissue_list[..., None] == jnp.arange(BR * BC, dtype=jnp.int32), axis=2)
    hits = hits.reshape(tiles_r, tiles_c, BR, BC).transpose(0, 2, 1, 3)
    return hits.reshape(tiles_r * BR, tiles_c * BC)


def exchange(sizes, views, send_sems, recv_sems, greet):
    n_r, n_c = sizes
    r, c = lax.axis_index("row"), lax.axis_index("col")

    def there(dr, dc):
        ok = None
        for at, step, n in ((r, dr, n_r), (c, dc, n_c)):
            if step == -1:
                one = at > 0
            elif step == 1:
                one = at < n - 1
            else:
                continue
            ok = one if ok is None else jnp.logical_and(ok, one)
        return ok

    def target(dr, dc):
        return {"row": r + dr, "col": c + dc}

    if greet:
        barrier = pltpu.get_barrier_semaphore()
        for dr, dc in SIDES:
            @pl.when(there(dr, dc))
            def _():
                pl.semaphore_signal(
                    barrier, inc=1, device_id=target(dr, dc), device_id_type=pl.DeviceIdType.MESH
                )

        peers = sum(there(dr, dc).astype(jnp.int32) for dr, dc in SIDES)
        pl.semaphore_wait(barrier, peers)

    def copy(k):
        dr, dc = SIDES[k]
        src, dst = views(dr, dc)
        return pltpu.make_async_remote_copy(
            src_ref=src,
            dst_ref=dst,
            send_sem=send_sems.at[k],
            recv_sem=recv_sems.at[k],
            device_id=target(dr, dc),
            device_id_type=pl.DeviceIdType.MESH,
        )

    for k, (dr, dc) in enumerate(SIDES):
        @pl.when(there(dr, dc))
        def _():
            copy(k).start()

    def finish():
        for k, (dr, dc) in enumerate(SIDES):
            @pl.when(there(dr, dc))
            def _():
                copy(k).wait_send()

            @pl.when(there(-dr, -dc))
            def _():
                copy(k).wait_recv()

    return finish


def token_views(blocks, frame):
    def span(step, n):
        if step == -1:
            return pl.ds(0, 1), pl.ds(n + 1, 1)
        if step == 1:
            return pl.ds(n - 1, 1), pl.ds(0, 1)
        return pl.ds(0, n), pl.ds(1, n)

    def views(dr, dc):
        (sr, tr), (sc, tc) = span(dr, BR), span(dc, BC)
        return blocks.at[sr, sc], frame.at[tr, tc]

    return views


def mixed_views(mixed, edges, top, bottom, sides, corners):
    height = mixed.shape[0]
    tall = edges.shape[1]

    def views(dr, dc):
        if dc == 0:
            if dr == -1:
                return mixed.at[pl.ds(0, 3)], bottom
            return mixed.at[pl.ds(height - 3, 3)], top
        mine = 0 if dc == -1 else 1
        if dr == 0:
            return edges.at[mine], sides.at[1 - mine]
        rows = pl.ds(0, 32) if dr == -1 else pl.ds(tall - 32, 32)
        place = (2 if dr == -1 else 0) + 1 - mine
        return edges.at[mine, rows], corners.at[place]

    return views


def attention_kernel(
    sizes,
    ok_ref,
    blocks,
    gain,
    w_qkv,
    w_out,
    bias,
    mixed,
    top,
    bottom,
    sides,
    corners,
    edges,
    frame,
    qkv,
    normed,
    att,
    mix,
    send_a,
    recv_a,
    send_b,
    recv_b,
):
    landed = exchange(sizes, token_views(blocks, frame), send_a, recv_a, True)
    width = frame.shape[-1]
    tok = BLK * BLK
    half = width // 2
    head = width // HEADS

    def norm(x, at):
        cent = x - jnp.mean(x, axis=-1, keepdims=True)
        var = jnp.mean(cent * cent, axis=-1, keepdims=True)
        y = cent * lax.rsqrt(var + 1e-06) * gain[...]
        normed[pl.ds(at * tok, tok), :] = y.astype(jnp.bfloat16)

    def halo(i, j):
        x = frame[i, j].astype(jnp.float32)
        return jnp.where(ok_ref[i, j] != 0, x, 0.0)

    def dots(i, at, cols_at, count, parts):
        rows = pl.ds(at * tok, count * tok)
        for n in parts:
            cols = pl.ds(n * width, width)
            p = jnp.dot(normed[rows, :], w_qkv[:, cols], preferred_element_type=jnp.float32)
            qkv[i, pl.ds(cols_at, count), :, cols] = p.astype(jnp.bfloat16).reshape(
                count, tok, width
            )

    def own_row(i, carry):
        for j in range(BC):
            norm(blocks[i, j].astype(jnp.float32), j)
        dots(i + 1, 0, 1, BC, range(3))
        return carry

    def halo_row(t, carry):
        i = t * (BR + 1)
        for j in range(BC + 2):
            norm(halo(i, j), j)
        dots(i, 0, 0, BC + 2, (1, 2))
        return carry

    def halo_columns():
        for t in range(2):
            j = t * (BC + 1)
            for i in range(BR):
                norm(halo(i + 1, j), t * BR + i)
        for n in (1, 2):
            cols = pl.ds(n * width, width)
            p = jnp.dot(
                normed[pl.ds(0, 2 * BR * tok), :],
                w_qkv[:, cols],
                preferred_element_type=jnp.float32,
            ).astype(jnp.bfloat16)
            for t in range(2):
                for i in range(BR):
                    k = (t * BR + i) * tok
                    qkv[i + 1, t * (BC + 1), :, cols] = p[k : k + tok]

    shape = (GROUP * tok, half)
    same = (
        lax.broadcasted_iota(jnp.int32, shape, 0) // tok
        == lax.broadcasted_iota(jnp.int32, shape, 1) // head
    )

    def attend(bi, bj):
        b = bi * BC + bj
        ok = ok_ref[bi + 1, bj + 1] != 0
        for g in range(2):
            q = qkv[bi + 1, bj + 1, :, pl.ds(g * half, half)].astype(jnp.float32)
            q = q * head ** (-0.5)
            q = jnp.where(same, jnp.concatenate([q] * GROUP, axis=0), 0.0)
            q = q.astype(jnp.bfloat16)

            def window(start):
                return jnp.concatenate(
                    [
                        qkv[bi + a, pl.ds(bj, 3), :, pl.ds(start, half)].reshape(
                            3 * tok, half
                        )
                        for a in range(3)
                    ],
                    axis=0,
                )

            s = lax.dot_general(
                q,
                window(width + g * half),
                (((1,), (1,)), ((), ())),
                preferred_element_type=jnp.float32,
            )
            s = s + bias[b]
            e = jnp.exp(s - jnp.max(s, axis=-1, keepdims=True))
            total = jnp.sum(e, axis=-1, keepdims=True)
            o = jnp.dot(
                e.astype(jnp.bfloat16),
                window(2 * width + g * half),
                preferred_element_type=jnp.float32,
            )
            o = jnp.where(same, o * (1.0 / total), 0.0)
            o = o[:tok] + o[tok : 2 * tok] + o[2 * tok : 3 * tok] + o[3 * tok :]
            o = jnp.where(ok, o, 0.0)
            att[b, :, pl.ds(g * half, half)] = o.astype(jnp.bfloat16)

    def loop(count, place):
        def step(t, carry):
            attend(*place(t))
            return carry

        lax.fori_loop(0, count, step, 0)

    def add(places):
        a = jnp.concatenate([att[bi * BC + bj] for bi, bj in places], axis=0)
        d = jnp.dot(a, w_out[...], preferred_element_type=jnp.float32)
        for n, (bi, bj) in enumerate(places):
            m = blocks[bi, bj].astype(jnp.float32) + d[n * tok : (n + 1) * tok]
            rows, cols = pl.ds(bi * BLK, BLK), pl.ds(bj * BLK, BLK)
            mix[rows, cols, :] = m.reshape(BLK, BLK, width)
            if bj in (0, BC - 1):
                edges[min(bj, 1), pl.ds(bi * tok, tok), :] = m.astype(jnp.bfloat16)

    def write(bi):
        rows = pl.ds(bi * BLK, BLK)
        mixed[rows] = mix[rows].astype(jnp.bfloat16)

    inner = BC - 2
    lax.fori_loop(0, BR, own_row, 0)
    loop(inner, lambda t: (1, 1 + t))
    landed()
    lax.fori_loop(0, 2, halo_row, 0)
    halo_columns()
    loop(BC, lambda t: (0, t))
    loop(BC, lambda t: (BR - 1, t))
    loop(2 * (BR - 2), lambda t: (1 + t // 2, (t % 2) * (BC - 1)))
    add([(0, j) for j in range(BC)])
    add([(BR - 1, j) for j in range(BC)])
    add([(i, j) for i in range(1, BR - 1) for j in (0, BC - 1)])
    write(0)
    write(BR - 1)
    views = mixed_views(mixed, edges, top, bottom, sides, corners)
    landed = exchange(sizes, views, send_b, recv_b, False)
    loop(inner * (BR - 3), lambda t: (2 + t // inner, 1 + t % inner))
    add([(i, j) for i in range(1, BR - 1) for j in range(1, BC - 1)])
    for i in range(1, BR - 1):
        write(i)
    landed()


def conv_kernel(
    flags, mixed, top, bottom, sides, corners, weight, bias, gain, out, framed, filt
):
    height, breadth, width = mixed.shape
    up, down, left, right = [flags[k] != 0 for k in range(4)]
    f32 = jnp.float32
    chunks = width // 128

    def put(rows, cols, v):
        for l in range(chunks):
            framed[l, rows, cols, :] = v[..., l * 128 : (l + 1) * 128]

    def fill(i, carry):
        rows = pl.ds(i * BLK, BLK)
        into = pl.ds(i * BLK + 3, BLK)
        put(into, pl.ds(8, breadth), mixed[rows].astype(f32))
        for k, ok, start in ((0, left, 0), (1, right, breadth + 8)):
            v = sides[k, pl.ds(i * BLK * 8, BLK * 8), :].astype(f32)
            put(into, pl.ds(start, 8), jnp.where(ok, v, 0.0).reshape(BLK, 8, width))
        return carry

    lax.fori_loop(0, height // BLK, fill, 0)
    for k, ok, ref, start in ((0, up, top, 0), (2, down, bottom, height + 3)):
        rows = pl.ds(start, 3)
        put(rows, pl.ds(8, breadth), jnp.where(ok, ref[...].astype(f32), 0.0))
        for h, side_ok, col in ((0, left, 0), (1, right, breadth + 8)):
            v = corners[k + h].astype(f32).reshape(4, 8, width)
            v = v[1:] if k == 0 else v[:3]
            both = jnp.logical_and(ok, side_ok)
            put(rows, pl.ds(col, 8), jnp.where(both, v, 0.0))

    def row_block(i, carry):
        r0 = i * BLK

        def lanes(l, inner):
            for c0 in range(0, breadth, 8):
                acc = jnp.zeros((BLK, 8, 128), f32) + bias[l]
                for dx in range(7):
                    v = framed[l, pl.ds(r0, BLK + 6), pl.ds(c0 + dx + 5, 8), :]
                    for dy in range(7):
                        acc = acc + v[dy : dy + BLK] * weight[l, dy * 7 + dx]
                filt[l, :, pl.ds(c0, 8), :] = acc
            return inner

        lax.fori_loop(0, chunks, lanes, 0)

        def norm(y, inner):
            f = jnp.concatenate([filt[l, y] for l in range(chunks)], axis=-1)
            cent = f - jnp.mean(f, axis=-1, keepdims=True)
            var = jnp.mean(cent * cent, axis=-1, keepdims=True)
            branch = cent * lax.rsqrt(var + 1e-06) * gain[...]
            out[r0 + y] = (mixed[r0 + y].astype(f32) + branch).astype(jnp.bfloat16)
            return inner

        lax.fori_loop(0, BLK, norm, 0)
        return carry

    lax.fori_loop(0, height // BLK, row_block, 0)


def per_device(tokens, tissue_list, ln_gain, w_qkv, w_out, conv_weight, conv_bias, conv_gain):
    height, breadth, width = tokens.shape
    tok = BLK * BLK
    bf16, f32 = jnp.bfloat16, jnp.float32
    sizes = (lax.axis_size("row"), lax.axis_size("col"))
    row, col = lax.axis_index("row"), lax.axis_index("col")
    dma = pltpu.SemaphoreType.DMA

    blocks = tokens.reshape(BR, BLK, BC, BLK, width).transpose(0, 2, 1, 3, 4)
    blocks = blocks.reshape(BR, BC, tok, width)
    table = jnp.pad(block_table(tissue_list), 1)
    near = lax.dynamic_slice(table, (row * BR, col * BC), (BR + 2, BC + 2))
    okay = jnp.stack(
        [near[a : a + BR, b : b + BC] for a in range(3) for b in range(3)], axis=-1
    ).reshape(BR * BC, 1, 9)
    bias = jnp.repeat(jnp.where(okay, 0.0, -1e30).astype(f32), tok, axis=-1)

    mixed, top, bottom, sides, corners = pl.pallas_call(
        functools.partial(attention_kernel, sizes),
        out_shape=(
            jax.ShapeDtypeStruct((height, breadth, width), bf16),
            jax.ShapeDtypeStruct((3, breadth, width), bf16),
            jax.ShapeDtypeStruct((3, breadth, width), bf16),
            jax.ShapeDtypeStruct((2, height * 8, width), bf16),
            jax.ShapeDtypeStruct((4, 32, width), bf16),
        ),
        in_specs=[SM] + [VM] * 5,
        out_specs=(VM,) + (ANY,) * 4,
        scratch_shapes=[
            pltpu.VMEM((2, height * 8, width), bf16),
            pltpu.VMEM((BR + 2, BC + 2, tok, width), bf16),
            pltpu.VMEM((BR + 2, BC + 2, tok, 3 * width), bf16),
            pltpu.VMEM(((BC + 2) * tok, width), bf16),
            pltpu.VMEM((BR * BC, tok, width), bf16),
            pltpu.VMEM((height, breadth, width), f32),
            dma((8,)),
            dma((8,)),
            dma((8,)),
            dma((8,)),
        ],
        compiler_params=pltpu.CompilerParams(
            vmem_limit_bytes=54 * MIB, collective_id=0, has_side_effects=True
        ),
    )(near.astype(jnp.int32), blocks, ln_gain.reshape(1, width), w_qkv, w_out, bias)

    flags = jnp.stack([row > 0, row < sizes[0] - 1, col > 0, col < sizes[1] - 1])
    chunks = width // 128
    weight = conv_weight.reshape(49, chunks, 1, 128).transpose(1, 0, 2, 3)
    weight = jnp.broadcast_to(weight, (chunks, 49, 8, 128))
    return pl.pallas_call(
        conv_kernel,
        out_shape=jax.ShapeDtypeStruct((height, breadth, width), bf16),
        in_specs=[SM] + [VM] * 8,
        out_specs=VM,
        scratch_shapes=[
            pltpu.VMEM((width // 128, height + 6, breadth + 16, 128), f32),
            pltpu.VMEM((width // 128, BLK, breadth, 128), f32),
        ],
        compiler_params=pltpu.CompilerParams(vmem_limit_bytes=40 * MIB),
    )(
        flags.astype(jnp.int32),
        mixed,
        top,
        bottom,
        sides,
        corners,
        weight,
        conv_bias.reshape(chunks, 1, 128),
        conv_gain.reshape(1, width),
    )


def solution(mesh):
    tile = P(("slide", "row"), "col", None)
    in_specs = (tile, P("slide", None, None), P(), P(), P(), P(), P(), P())
    return jax.shard_map(
        per_device, mesh=mesh, in_specs=in_specs, out_specs=tile, check_vma=False
    )
```

```python
import functools

import jax
import jax.numpy as jnp
from jax import lax
from jax.experimental import pallas as pl
from jax.experimental.pallas import tpu as pltpu
from jax.sharding import PartitionSpec as P

HEADS = 8
BLK = 8
BR = 4
BC = 8
GROUP = 4
SIDES = ((-1, 0), (1, 0), (0, -1), (0, 1), (-1, -1), (-1, 1), (1, -1), (1, 1))
VM = pl.BlockSpec(memory_space=pltpu.VMEM)
SM = pl.BlockSpec(memory_space=pltpu.SMEM)
ANY = pl.BlockSpec(memory_space=pl.ANY)
MIB = 1024 * 1024


def block_table(tissue_list):
    tiles_r, tiles_c, slots = tissue_list.shape
    hits = jnp.any(tissue_list[..., None] == jnp.arange(BR * BC, dtype=jnp.int32), axis=2)
    hits = hits.reshape(tiles_r, tiles_c, BR, BC).transpose(0, 2, 1, 3)
    return hits.reshape(tiles_r * BR, tiles_c * BC)


def exchange(sizes, views, send_sems, recv_sems, greet):
    n_r, n_c = sizes
    r, c = lax.axis_index("row"), lax.axis_index("col")

    def there(dr, dc):
        ok = None
        for at, step, n in ((r, dr, n_r), (c, dc, n_c)):
            if step == -1:
                one = at > 0
            elif step == 1:
                one = at < n - 1
            else:
                continue
            ok = one if ok is None else jnp.logical_and(ok, one)
        return ok

    def target(dr, dc):
        return {"row": r + dr, "col": c + dc}

    if greet:
        barrier = pltpu.get_barrier_semaphore()
        for dr, dc in SIDES:
            @pl.when(there(dr, dc))
            def _():
                pl.semaphore_signal(
                    barrier, inc=1, device_id=target(dr, dc), device_id_type=pl.DeviceIdType.MESH
                )

        peers = sum(there(dr, dc).astype(jnp.int32) for dr, dc in SIDES)
        pl.semaphore_wait(barrier, peers)

    def copy(k):
        dr, dc = SIDES[k]
        src, dst = views(dr, dc)
        return pltpu.make_async_remote_copy(
            src_ref=src,
            dst_ref=dst,
            send_sem=send_sems.at[k],
            recv_sem=recv_sems.at[k],
            device_id=target(dr, dc),
            device_id_type=pl.DeviceIdType.MESH,
        )

    for k, (dr, dc) in enumerate(SIDES):
        @pl.when(there(dr, dc))
        def _():
            copy(k).start()

    def finish():
        for k, (dr, dc) in enumerate(SIDES):
            @pl.when(there(dr, dc))
            def _():
                copy(k).wait_send()

            @pl.when(there(-dr, -dc))
            def _():
                copy(k).wait_recv()

    return finish


def token_views(blocks, frame):
    def span(step, n):
        if step == -1:
            return pl.ds(0, 1), pl.ds(n + 1, 1)
        if step == 1:
            return pl.ds(n - 1, 1), pl.ds(0, 1)
        return pl.ds(0, n), pl.ds(1, n)

    def views(dr, dc):
        (sr, tr), (sc, tc) = span(dr, BR), span(dc, BC)
        return blocks.at[sr, sc], frame.at[tr, tc]

    return views


def mixed_views(mixed, edges, top, bottom, sides, corners):
    height = mixed.shape[0]
    tall = edges.shape[1]

    def views(dr, dc):
        if dc == 0:
            if dr == -1:
                return mixed.at[pl.ds(0, 3)], bottom
            return mixed.at[pl.ds(height - 3, 3)], top
        mine = 0 if dc == -1 else 1
        if dr == 0:
            return edges.at[mine], sides.at[1 - mine]
        rows = pl.ds(0, 32) if dr == -1 else pl.ds(tall - 32, 32)
        place = (2 if dr == -1 else 0) + 1 - mine
        return edges.at[mine, rows], corners.at[place]

    return views


def attention_kernel(
    sizes,
    ok_ref,
    blocks,
    gain,
    w_qkv,
    w_out,
    bias,
    mixed,
    top,
    bottom,
    sides,
    corners,
    edges,
    frame,
    qkv,
    normed,
    att,
    mix,
    send_a,
    recv_a,
    send_b,
    recv_b,
):
    landed = exchange(sizes, token_views(blocks, frame), send_a, recv_a, True)
    width = frame.shape[-1]
    tok = BLK * BLK
    half = width // 2
    head = width // HEADS

    def norm(x, at):
        cent = x - jnp.mean(x, axis=-1, keepdims=True)
        var = jnp.mean(cent * cent, axis=-1, keepdims=True)
        y = cent * lax.rsqrt(var + 1e-06) * gain[...]
        normed[pl.ds(at * tok, tok), :] = y.astype(jnp.bfloat16)

    def halo(i, j):
        x = frame[i, j].astype(jnp.float32)
        return jnp.where(ok_ref[i, j] != 0, x, 0.0)

    def dots(i, at, cols_at, count, parts):
        rows = pl.ds(at * tok, count * tok)
        for n in parts:
            cols = pl.ds(n * width, width)
            p = jnp.dot(normed[rows, :], w_qkv[:, cols], preferred_element_type=jnp.float32)
            qkv[i, pl.ds(cols_at, count), :, cols] = p.astype(jnp.bfloat16).reshape(
                count, tok, width
            )

    def own_row(i, carry):
        for j in range(BC):
            norm(blocks[i, j].astype(jnp.float32), j)
        dots(i + 1, 0, 1, BC, range(3))
        return carry

    def halo_row(t, carry):
        i = t * (BR + 1)
        for j in range(BC + 2):
            norm(halo(i, j), j)
        dots(i, 0, 0, BC + 2, (1, 2))
        return carry

    def halo_columns():
        for t in range(2):
            j = t * (BC + 1)
            for i in range(BR):
                norm(halo(i + 1, j), t * BR + i)
        for n in (1, 2):
            cols = pl.ds(n * width, width)
            p = jnp.dot(
                normed[pl.ds(0, 2 * BR * tok), :],
                w_qkv[:, cols],
                preferred_element_type=jnp.float32,
            ).astype(jnp.bfloat16)
            for t in range(2):
                for i in range(BR):
                    k = (t * BR + i) * tok
                    qkv[i + 1, t * (BC + 1), :, cols] = p[k : k + tok]

    shape = (GROUP * tok, half)
    same = (
        lax.broadcasted_iota(jnp.int32, shape, 0) // tok
        == lax.broadcasted_iota(jnp.int32, shape, 1) // head
    )

    def window(bi, bj, start):
        return jnp.concatenate(
            [
                qkv[bi + a, pl.ds(bj, 3), :, pl.ds(start, half)].reshape(3 * tok, half)
                for a in range(3)
            ],
            axis=0,
        )

    def score(bi, bj, g):
        q = qkv[bi + 1, bj + 1, :, pl.ds(g * half, half)].astype(jnp.float32)
        q = q * head ** (-0.5)
        q = jnp.where(same, jnp.concatenate([q] * GROUP, axis=0), 0.0)
        return lax.dot_general(
            q.astype(jnp.bfloat16),
            window(bi, bj, width + g * half),
            (((1,), (1,)), ((), ())),
            preferred_element_type=jnp.float32,
        )

    def blend(bi, bj, g, s):
        b = bi * BC + bj
        s = s + bias[b]
        e = jnp.exp(s - jnp.max(s, axis=-1, keepdims=True))
        total = jnp.sum(e, axis=-1, keepdims=True)
        o = jnp.dot(
            e.astype(jnp.bfloat16),
            window(bi, bj, 2 * width + g * half),
            preferred_element_type=jnp.float32,
        )
        o = jnp.where(same, o * (1.0 / total), 0.0)
        o = o[:tok] + o[tok : 2 * tok] + o[2 * tok : 3 * tok] + o[3 * tok :]
        o = jnp.where(ok_ref[bi + 1, bj + 1] != 0, o, 0.0)
        att[b, :, pl.ds(g * half, half)] = o.astype(jnp.bfloat16)

    def loop(count, place):
        def step(t, carry):
            jobs = [(*place(2 * t + k), g) for k in range(2) for g in range(2)]
            s = score(*jobs[0])
            for n, job in enumerate(jobs):
                ahead = score(*jobs[n + 1]) if n + 1 < len(jobs) else None
                blend(*job, s)
                s = ahead
            return carry

        lax.fori_loop(0, count // 2, step, 0)

    def add(places):
        a = jnp.concatenate([att[bi * BC + bj] for bi, bj in places], axis=0)
        d = jnp.dot(a, w_out[...], preferred_element_type=jnp.float32)
        for n, (bi, bj) in enumerate(places):
            m = blocks[bi, bj].astype(jnp.float32) + d[n * tok : (n + 1) * tok]
            rows, cols = pl.ds(bi * BLK, BLK), pl.ds(bj * BLK, BLK)
            mix[rows, cols, :] = m.reshape(BLK, BLK, width)
            if bj in (0, BC - 1):
                edges[min(bj, 1), pl.ds(bi * tok, tok), :] = m.astype(jnp.bfloat16)

    def write(bi):
        rows = pl.ds(bi * BLK, BLK)
        mixed[rows] = mix[rows].astype(jnp.bfloat16)

    inner = BC - 2
    lax.fori_loop(0, BR, own_row, 0)
    loop(inner, lambda t: (1, 1 + t))
    landed()
    lax.fori_loop(0, 2, halo_row, 0)
    halo_columns()
    loop(BC, lambda t: (0, t))
    loop(BC, lambda t: (BR - 1, t))
    loop(2 * (BR - 2), lambda t: (1 + t // 2, (t % 2) * (BC - 1)))
    add([(0, j) for j in range(BC)])
    add([(BR - 1, j) for j in range(BC)])
    add([(i, j) for i in range(1, BR - 1) for j in (0, BC - 1)])
    write(0)
    write(BR - 1)
    views = mixed_views(mixed, edges, top, bottom, sides, corners)
    landed = exchange(sizes, views, send_b, recv_b, False)
    loop(inner * (BR - 3), lambda t: (2 + t // inner, 1 + t % inner))
    add([(i, j) for i in range(1, BR - 1) for j in range(1, BC - 1)])
    for i in range(1, BR - 1):
        write(i)
    landed()


def conv_kernel(
    flags, mixed, top, bottom, sides, corners, weight, bias, gain, out, framed, filt
):
    height, breadth, width = mixed.shape
    up, down, left, right = [flags[k] != 0 for k in range(4)]
    f32 = jnp.float32
    chunks = width // 128

    def put(rows, cols, v):
        for l in range(chunks):
            framed[l, rows, cols, :] = v[..., l * 128 : (l + 1) * 128]

    def fill(i, carry):
        rows = pl.ds(i * BLK, BLK)
        into = pl.ds(i * BLK + 3, BLK)
        put(into, pl.ds(8, breadth), mixed[rows].astype(f32))
        for k, ok, start in ((0, left, 0), (1, right, breadth + 8)):
            v = sides[k, pl.ds(i * BLK * 8, BLK * 8), :].astype(f32)
            put(into, pl.ds(start, 8), jnp.where(ok, v, 0.0).reshape(BLK, 8, width))
        return carry

    lax.fori_loop(0, height // BLK, fill, 0)
    for k, ok, ref, start in ((0, up, top, 0), (2, down, bottom, height + 3)):
        rows = pl.ds(start, 3)
        put(rows, pl.ds(8, breadth), jnp.where(ok, ref[...].astype(f32), 0.0))
        for h, side_ok, col in ((0, left, 0), (1, right, breadth + 8)):
            v = corners[k + h].astype(f32).reshape(4, 8, width)
            v = v[1:] if k == 0 else v[:3]
            both = jnp.logical_and(ok, side_ok)
            put(rows, pl.ds(col, 8), jnp.where(both, v, 0.0))

    def row_block(i, carry):
        r0 = i * BLK

        def lanes(l, inner):
            for c0 in range(0, breadth, 8):
                acc = jnp.zeros((BLK, 8, 128), f32) + bias[l]
                for dx in range(7):
                    v = framed[l, pl.ds(r0, BLK + 6), pl.ds(c0 + dx + 5, 8), :]
                    for dy in range(7):
                        acc = acc + v[dy : dy + BLK] * weight[l, dy * 7 + dx]
                filt[l, :, pl.ds(c0, 8), :] = acc
            return inner

        lax.fori_loop(0, chunks, lanes, 0)

        def norm(t, inner):
            for y in range(4):
                y = t * 4 + y
                f = jnp.concatenate([filt[l, y] for l in range(chunks)], axis=-1)
                cent = f - jnp.mean(f, axis=-1, keepdims=True)
                var = jnp.mean(cent * cent, axis=-1, keepdims=True)
                branch = cent * lax.rsqrt(var + 1e-06) * gain[...]
                out[r0 + y] = (mixed[r0 + y].astype(f32) + branch).astype(jnp.bfloat16)
            return inner

        lax.fori_loop(0, BLK // 4, norm, 0)
        return carry

    lax.fori_loop(0, height // BLK, row_block, 0)


def per_device(tokens, tissue_list, ln_gain, w_qkv, w_out, conv_weight, conv_bias, conv_gain):
    height, breadth, width = tokens.shape
    tok = BLK * BLK
    bf16, f32 = jnp.bfloat16, jnp.float32
    sizes = (lax.axis_size("row"), lax.axis_size("col"))
    row, col = lax.axis_index("row"), lax.axis_index("col")
    dma = pltpu.SemaphoreType.DMA

    blocks = tokens.reshape(BR, BLK, BC, BLK, width).transpose(0, 2, 1, 3, 4)
    blocks = blocks.reshape(BR, BC, tok, width)
    table = jnp.pad(block_table(tissue_list), 1)
    near = lax.dynamic_slice(table, (row * BR, col * BC), (BR + 2, BC + 2))
    okay = jnp.stack(
        [near[a : a + BR, b : b + BC] for a in range(3) for b in range(3)], axis=-1
    ).reshape(BR * BC, 1, 9)
    bias = jnp.repeat(jnp.where(okay, 0.0, -1e30).astype(f32), tok, axis=-1)

    mixed, top, bottom, sides, corners = pl.pallas_call(
        functools.partial(attention_kernel, sizes),
        out_shape=(
            jax.ShapeDtypeStruct((height, breadth, width), bf16),
            jax.ShapeDtypeStruct((3, breadth, width), bf16),
            jax.ShapeDtypeStruct((3, breadth, width), bf16),
            jax.ShapeDtypeStruct((2, height * 8, width), bf16),
            jax.ShapeDtypeStruct((4, 32, width), bf16),
        ),
        in_specs=[SM] + [VM] * 5,
        out_specs=(VM,) * 5,
        scratch_shapes=[
            pltpu.VMEM((2, height * 8, width), bf16),
            pltpu.VMEM((BR + 2, BC + 2, tok, width), bf16),
            pltpu.VMEM((BR + 2, BC + 2, tok, 3 * width), bf16),
            pltpu.VMEM(((BC + 2) * tok, width), bf16),
            pltpu.VMEM((BR * BC, tok, width), bf16),
            pltpu.VMEM((height, breadth, width), f32),
            dma((8,)),
            dma((8,)),
            dma((8,)),
            dma((8,)),
        ],
        compiler_params=pltpu.CompilerParams(
            vmem_limit_bytes=54 * MIB, collective_id=0, has_side_effects=True
        ),
    )(near.astype(jnp.int32), blocks, ln_gain.reshape(1, width), w_qkv, w_out, bias)

    flags = jnp.stack([row > 0, row < sizes[0] - 1, col > 0, col < sizes[1] - 1])
    chunks = width // 128
    weight = conv_weight.reshape(49, chunks, 1, 128).transpose(1, 0, 2, 3)
    weight = jnp.broadcast_to(weight, (chunks, 49, 8, 128))
    return pl.pallas_call(
        conv_kernel,
        out_shape=jax.ShapeDtypeStruct((height, breadth, width), bf16),
        in_specs=[SM] + [VM] * 8,
        out_specs=VM,
        scratch_shapes=[
            pltpu.VMEM((width // 128, height + 6, breadth + 16, 128), f32),
            pltpu.VMEM((width // 128, BLK, breadth, 128), f32),
        ],
        compiler_params=pltpu.CompilerParams(vmem_limit_bytes=40 * MIB),
    )(
        flags.astype(jnp.int32),
        mixed,
        top,
        bottom,
        sides,
        corners,
        weight,
        conv_bias.reshape(chunks, 1, 128),
        conv_gain.reshape(1, width),
    )


def solution(mesh):
    tile = P(("slide", "row"), "col", None)
    in_specs = (tile, P("slide", None, None), P(), P(), P(), P(), P(), P())
    return jax.shard_map(
        per_device, mesh=mesh, in_specs=in_specs, out_specs=tile, check_vma=False
    )
```

```python
import functools

import jax
import jax.numpy as jnp
from jax import lax
from jax.experimental import pallas as pl
from jax.experimental.pallas import tpu as pltpu
from jax.sharding import PartitionSpec as P

HEADS = 8
BLK = 8
BR = 4
BC = 8
GROUP = 4
SIDES = ((-1, 0), (1, 0), (0, -1), (0, 1), (-1, -1), (-1, 1), (1, -1), (1, 1))
VM = pl.BlockSpec(memory_space=pltpu.VMEM)
SM = pl.BlockSpec(memory_space=pltpu.SMEM)
ANY = pl.BlockSpec(memory_space=pl.ANY)
MIB = 1024 * 1024


def block_table(tissue_list):
    tiles_r, tiles_c, slots = tissue_list.shape
    hits = jnp.any(tissue_list[..., None] == jnp.arange(BR * BC, dtype=jnp.int32), axis=2)
    hits = hits.reshape(tiles_r, tiles_c, BR, BC).transpose(0, 2, 1, 3)
    return hits.reshape(tiles_r * BR, tiles_c * BC)


def exchange(sizes, views, send_sems, recv_sems, greet):
    n_r, n_c = sizes
    r, c = lax.axis_index("row"), lax.axis_index("col")

    def there(dr, dc):
        ok = None
        for at, step, n in ((r, dr, n_r), (c, dc, n_c)):
            if step == -1:
                one = at > 0
            elif step == 1:
                one = at < n - 1
            else:
                continue
            ok = one if ok is None else jnp.logical_and(ok, one)
        return ok

    def target(dr, dc):
        return {"row": r + dr, "col": c + dc}

    if greet:
        barrier = pltpu.get_barrier_semaphore()
        for dr, dc in SIDES:
            @pl.when(there(dr, dc))
            def _():
                pl.semaphore_signal(
                    barrier, inc=1, device_id=target(dr, dc), device_id_type=pl.DeviceIdType.MESH
                )

        peers = sum(there(dr, dc).astype(jnp.int32) for dr, dc in SIDES)
        pl.semaphore_wait(barrier, peers)

    def copy(k):
        dr, dc = SIDES[k]
        src, dst = views(dr, dc)
        return pltpu.make_async_remote_copy(
            src_ref=src,
            dst_ref=dst,
            send_sem=send_sems.at[k],
            recv_sem=recv_sems.at[k],
            device_id=target(dr, dc),
            device_id_type=pl.DeviceIdType.MESH,
        )

    for k, (dr, dc) in enumerate(SIDES):
        @pl.when(there(dr, dc))
        def _():
            copy(k).start()

    def finish():
        for k, (dr, dc) in enumerate(SIDES):
            @pl.when(there(dr, dc))
            def _():
                copy(k).wait_send()

            @pl.when(there(-dr, -dc))
            def _():
                copy(k).wait_recv()

    return finish


def token_views(blocks, frame):
    def span(step, n):
        if step == -1:
            return pl.ds(0, 1), pl.ds(n + 1, 1)
        if step == 1:
            return pl.ds(n - 1, 1), pl.ds(0, 1)
        return pl.ds(0, n), pl.ds(1, n)

    def views(dr, dc):
        (sr, tr), (sc, tc) = span(dr, BR), span(dc, BC)
        return blocks.at[sr, sc], frame.at[tr, tc]

    return views


def mixed_views(mixed, edges, top, bottom, sides, corners):
    height = mixed.shape[0]
    tall = edges.shape[1]

    def views(dr, dc):
        if dc == 0:
            if dr == -1:
                return mixed.at[pl.ds(0, 3)], bottom
            return mixed.at[pl.ds(height - 3, 3)], top
        mine = 0 if dc == -1 else 1
        if dr == 0:
            return edges.at[mine], sides.at[1 - mine]
        rows = pl.ds(0, 32) if dr == -1 else pl.ds(tall - 32, 32)
        place = (2 if dr == -1 else 0) + 1 - mine
        return edges.at[mine, rows], corners.at[place]

    return views


def attention_kernel(
    sizes,
    ok_ref,
    tokens,
    gain,
    w_qkv,
    w_out,
    bias,
    mixed,
    top,
    bottom,
    sides,
    corners,
    edges,
    blocks,
    frame,
    qkv,
    normed,
    att,
    mix,
    send_a,
    recv_a,
    send_b,
    recv_b,
):
    def cut(bi, carry):
        for pair in range(BC // 2):
            x = tokens[pl.ds(bi * BLK, BLK), pl.ds(pair * 2 * BLK, 2 * BLK), :]
            x = x.astype(jnp.float32).reshape(BLK, 2, BLK, x.shape[-1])
            for k in range(2):
                part = x[:, k].reshape(BLK * BLK, x.shape[-1])
                blocks[bi, 2 * pair + k] = part.astype(jnp.bfloat16)
        return carry

    lax.fori_loop(0, BR, cut, 0)
    landed = exchange(sizes, token_views(blocks, frame), send_a, recv_a, True)
    width = frame.shape[-1]
    tok = BLK * BLK
    half = width // 2
    head = width // HEADS

    def norm(x, at):
        cent = x - jnp.mean(x, axis=-1, keepdims=True)
        var = jnp.mean(cent * cent, axis=-1, keepdims=True)
        y = cent * lax.rsqrt(var + 1e-06) * gain[...]
        normed[pl.ds(at * tok, tok), :] = y.astype(jnp.bfloat16)

    def halo(i, j):
        x = frame[i, j].astype(jnp.float32)
        return jnp.where(ok_ref[i, j] != 0, x, 0.0)

    def dots(i, at, cols_at, count, parts):
        rows = pl.ds(at * tok, count * tok)
        for n in parts:
            cols = pl.ds(n * width, width)
            p = jnp.dot(normed[rows, :], w_qkv[:, cols], preferred_element_type=jnp.float32)
            qkv[i, pl.ds(cols_at, count), :, cols] = p.astype(jnp.bfloat16).reshape(
                count, tok, width
            )

    def own_row(i, carry):
        for j in range(BC):
            norm(blocks[i, j].astype(jnp.float32), j)
        dots(i + 1, 0, 1, BC, range(3))
        return carry

    def halo_row(t, carry):
        i = t * (BR + 1)
        for j in range(BC + 2):
            norm(halo(i, j), j)
        dots(i, 0, 0, BC + 2, (1, 2))
        return carry

    def halo_columns():
        for t in range(2):
            j = t * (BC + 1)
            for i in range(BR):
                norm(halo(i + 1, j), t * BR + i)
        for n in (1, 2):
            cols = pl.ds(n * width, width)
            p = jnp.dot(
                normed[pl.ds(0, 2 * BR * tok), :],
                w_qkv[:, cols],
                preferred_element_type=jnp.float32,
            ).astype(jnp.bfloat16)
            for t in range(2):
                for i in range(BR):
                    k = (t * BR + i) * tok
                    qkv[i + 1, t * (BC + 1), :, cols] = p[k : k + tok]

    shape = (GROUP * tok, half)
    same = (
        lax.broadcasted_iota(jnp.int32, shape, 0) // tok
        == lax.broadcasted_iota(jnp.int32, shape, 1) // head
    )

    def window(bi, bj, start):
        return jnp.concatenate(
            [
                qkv[bi + a, pl.ds(bj, 3), :, pl.ds(start, half)].reshape(3 * tok, half)
                for a in range(3)
            ],
            axis=0,
        )

    def score(bi, bj, g):
        q = qkv[bi + 1, bj + 1, :, pl.ds(g * half, half)].astype(jnp.float32)
        q = q * head ** (-0.5)
        q = jnp.where(same, jnp.concatenate([q] * GROUP, axis=0), 0.0)
        return lax.dot_general(
            q.astype(jnp.bfloat16),
            window(bi, bj, width + g * half),
            (((1,), (1,)), ((), ())),
            preferred_element_type=jnp.float32,
        )

    def blend(bi, bj, g, s):
        b = bi * BC + bj
        s = s + bias[b]
        e = jnp.exp(s - jnp.max(s, axis=-1, keepdims=True))
        total = jnp.sum(e, axis=-1, keepdims=True)
        o = jnp.dot(
            e.astype(jnp.bfloat16),
            window(bi, bj, 2 * width + g * half),
            preferred_element_type=jnp.float32,
        )
        o = jnp.where(same, o * (1.0 / total), 0.0)
        o = o[:tok] + o[tok : 2 * tok] + o[2 * tok : 3 * tok] + o[3 * tok :]
        o = jnp.where(ok_ref[bi + 1, bj + 1] != 0, o, 0.0)
        att[b, :, pl.ds(g * half, half)] = o.astype(jnp.bfloat16)

    def loop(count, place):
        def step(t, carry):
            jobs = [(*place(2 * t + k), g) for k in range(2) for g in range(2)]
            s = score(*jobs[0])
            for n, job in enumerate(jobs):
                ahead = score(*jobs[n + 1]) if n + 1 < len(jobs) else None
                blend(*job, s)
                s = ahead
            return carry

        lax.fori_loop(0, count // 2, step, 0)

    def add(places):
        a = jnp.concatenate([att[bi * BC + bj] for bi, bj in places], axis=0)
        d = jnp.dot(a, w_out[...], preferred_element_type=jnp.float32)
        for n, (bi, bj) in enumerate(places):
            m = blocks[bi, bj].astype(jnp.float32) + d[n * tok : (n + 1) * tok]
            rows, cols = pl.ds(bi * BLK, BLK), pl.ds(bj * BLK, BLK)
            mix[rows, cols, :] = m.reshape(BLK, BLK, width)
            if bj in (0, BC - 1):
                edges[min(bj, 1), pl.ds(bi * tok, tok), :] = m.astype(jnp.bfloat16)

    def write(bi):
        rows = pl.ds(bi * BLK, BLK)
        mixed[rows] = mix[rows].astype(jnp.bfloat16)

    inner = BC - 2
    lax.fori_loop(0, BR, own_row, 0)
    loop(inner, lambda t: (1, 1 + t))
    landed()
    lax.fori_loop(0, 2, halo_row, 0)
    halo_columns()
    loop(BC, lambda t: (0, t))
    loop(BC, lambda t: (BR - 1, t))
    loop(2 * (BR - 2), lambda t: (1 + t // 2, (t % 2) * (BC - 1)))
    add([(0, j) for j in range(BC)])
    add([(BR - 1, j) for j in range(BC)])
    add([(i, j) for i in range(1, BR - 1) for j in (0, BC - 1)])
    write(0)
    write(BR - 1)
    views = mixed_views(mixed, edges, top, bottom, sides, corners)
    landed = exchange(sizes, views, send_b, recv_b, False)
    loop(inner * (BR - 3), lambda t: (2 + t // inner, 1 + t % inner))
    add([(i, j) for i in range(1, BR - 1) for j in range(1, BC - 1)])
    for i in range(1, BR - 1):
        write(i)
    landed()


def conv_kernel(
    flags, mixed, top, bottom, sides, corners, weight, bias, gain, out, framed, filt
):
    height, breadth, width = mixed.shape
    up, down, left, right = [flags[k] != 0 for k in range(4)]
    f32 = jnp.float32
    chunks = width // 128

    def put(rows, cols, v):
        for l in range(chunks):
            framed[l, rows, cols, :] = v[..., l * 128 : (l + 1) * 128]

    def fill(i, carry):
        rows = pl.ds(i * BLK, BLK)
        into = pl.ds(i * BLK + 3, BLK)
        put(into, pl.ds(8, breadth), mixed[rows].astype(f32))
        for k, ok, start in ((0, left, 0), (1, right, breadth + 8)):
            v = sides[k, pl.ds(i * BLK * 8, BLK * 8), :].astype(f32)
            put(into, pl.ds(start, 8), jnp.where(ok, v, 0.0).reshape(BLK, 8, width))
        return carry

    lax.fori_loop(0, height // BLK, fill, 0)
    for k, ok, ref, start in ((0, up, top, 0), (2, down, bottom, height + 3)):
        rows = pl.ds(start, 3)
        put(rows, pl.ds(8, breadth), jnp.where(ok, ref[...].astype(f32), 0.0))
        for h, side_ok, col in ((0, left, 0), (1, right, breadth + 8)):
            v = corners[k + h].astype(f32).reshape(4, 8, width)
            v = v[1:] if k == 0 else v[:3]
            both = jnp.logical_and(ok, side_ok)
            put(rows, pl.ds(col, 8), jnp.where(both, v, 0.0))

    def row_block(i, carry):
        r0 = i * BLK

        def lanes(l, inner):
            for c0 in range(0, breadth, 8):
                acc = jnp.zeros((BLK, 8, 128), f32) + bias[l]
                for dx in range(7):
                    v = framed[l, pl.ds(r0, BLK + 6), pl.ds(c0 + dx + 5, 8), :]
                    for dy in range(7):
                        acc = acc + v[dy : dy + BLK] * weight[l, dy * 7 + dx]
                filt[l, :, pl.ds(c0, 8), :] = acc
            return inner

        lax.fori_loop(0, chunks, lanes, 0)

        def norm(t, inner):
            for y in range(4):
                y = t * 4 + y
                f = jnp.concatenate([filt[l, y] for l in range(chunks)], axis=-1)
                cent = f - jnp.mean(f, axis=-1, keepdims=True)
                var = jnp.mean(cent * cent, axis=-1, keepdims=True)
                branch = cent * lax.rsqrt(var + 1e-06) * gain[...]
                out[r0 + y] = (mixed[r0 + y].astype(f32) + branch).astype(jnp.bfloat16)
            return inner

        lax.fori_loop(0, BLK // 4, norm, 0)
        return carry

    lax.fori_loop(0, height // BLK, row_block, 0)


def per_device(tokens, tissue_list, ln_gain, w_qkv, w_out, conv_weight, conv_bias, conv_gain):
    height, breadth, width = tokens.shape
    tok = BLK * BLK
    bf16, f32 = jnp.bfloat16, jnp.float32
    sizes = (lax.axis_size("row"), lax.axis_size("col"))
    row, col = lax.axis_index("row"), lax.axis_index("col")
    dma = pltpu.SemaphoreType.DMA

    table = jnp.pad(block_table(tissue_list), 1)
    near = lax.dynamic_slice(table, (row * BR, col * BC), (BR + 2, BC + 2))
    okay = jnp.stack(
        [near[a : a + BR, b : b + BC] for a in range(3) for b in range(3)], axis=-1
    ).reshape(BR * BC, 1, 9)
    bias = jnp.repeat(jnp.where(okay, 0.0, -1e30).astype(f32), tok, axis=-1)

    mixed, top, bottom, sides, corners = pl.pallas_call(
        functools.partial(attention_kernel, sizes),
        out_shape=(
            jax.ShapeDtypeStruct((height, breadth, width), bf16),
            jax.ShapeDtypeStruct((3, breadth, width), bf16),
            jax.ShapeDtypeStruct((3, breadth, width), bf16),
            jax.ShapeDtypeStruct((2, height * 8, width), bf16),
            jax.ShapeDtypeStruct((4, 32, width), bf16),
        ),
        in_specs=[SM] + [VM] * 5,
        out_specs=(VM,) * 5,
        scratch_shapes=[
            pltpu.VMEM((2, height * 8, width), bf16),
            pltpu.VMEM((BR, BC, tok, width), bf16),
            pltpu.VMEM((BR + 2, BC + 2, tok, width), bf16),
            pltpu.VMEM((BR + 2, BC + 2, tok, 3 * width), bf16),
            pltpu.VMEM(((BC + 2) * tok, width), bf16),
            pltpu.VMEM((BR * BC, tok, width), bf16),
            pltpu.VMEM((height, breadth, width), f32),
            dma((8,)),
            dma((8,)),
            dma((8,)),
            dma((8,)),
        ],
        compiler_params=pltpu.CompilerParams(
            vmem_limit_bytes=54 * MIB, collective_id=0, has_side_effects=True
        ),
    )(near.astype(jnp.int32), tokens, ln_gain.reshape(1, width), w_qkv, w_out, bias)

    flags = jnp.stack([row > 0, row < sizes[0] - 1, col > 0, col < sizes[1] - 1])
    chunks = width // 128
    weight = conv_weight.reshape(49, chunks, 1, 128).transpose(1, 0, 2, 3)
    weight = jnp.broadcast_to(weight, (chunks, 49, 8, 128))
    return pl.pallas_call(
        conv_kernel,
        out_shape=jax.ShapeDtypeStruct((height, breadth, width), bf16),
        in_specs=[SM] + [VM] * 8,
        out_specs=VM,
        scratch_shapes=[
            pltpu.VMEM((width // 128, height + 6, breadth + 16, 128), f32),
            pltpu.VMEM((width // 128, BLK, breadth, 128), f32),
        ],
        compiler_params=pltpu.CompilerParams(vmem_limit_bytes=40 * MIB),
    )(
        flags.astype(jnp.int32),
        mixed,
        top,
        bottom,
        sides,
        corners,
        weight,
        conv_bias.reshape(chunks, 1, 128),
        conv_gain.reshape(1, width),
    )


def solution(mesh):
    tile = P(("slide", "row"), "col", None)
    in_specs = (tile, P("slide", None, None), P(), P(), P(), P(), P(), P())
    return jax.shard_map(
        per_device, mesh=mesh, in_specs=in_specs, out_specs=tile, check_vma=False
    )
```
